32 devices in a mesh: src: 2 (over y), tile: 16 (over z, x, core).
Axes of the slice: x: 2, y: 2, z: 4, core: 2. Of those that a mesh axis runs over, the one named last changes fastest.
Arguments:
- mask_tiles: bfloat16 [16, 1024, 1024], P('tile'), may hold values from -6 to 6
- slot_pos: int32 [16], replicated, may hold values from 0 to 15, as said below
- src_shift: int32 [4, 2], P('src'), may hold values from -32 to 32
- src_weight: int32 [4], P('src'), may hold values from 1 to 8
- pupil_phase: float32 [128, 128], replicated, may hold values from -3.140625 to 3.140625
- target: bfloat16 [16, 1024, 1024], P('tile'), may hold values from 0 to 1
Outputs:
- resist: float32 [16, 1024, 1024], P('tile', 'src')
- mask_step: float32 [16, 1024, 1024], P('tile', 'src')
The draws below stay inside these ranges and needn't reach their ends.
Inputs may be any that keep to these rules, and one draw needn't show every extreme that they name: slot_pos is a permutation of the strip positions.
All inputs are finite; a program needn't handle non-finite values.
Results may differ from the reference program's by a relative error of at most 0.0051.
Values may be sent and summed in bfloat16 or wider, within the bound.
A program may use at most 128 MiB of HBM per device.

```python
import math
import jax
import jax.numpy as jnp
from jax import lax

TILE_PX = 1024
HALO = 64
FREQ = 128
PUPIL_R = 28
SHIFT_MAX = 32
SOURCES = 4
TILES = 16
EXT_PX = 1152


def draw_slot_pos(key, part):
    order_key = jax.random.fold_in(key, 11)
    pick_key = jax.random.fold_in(key, 23)
    order = jax.random.permutation(order_key, TILES).astype(jnp.int32)
    half_count = TILES // 2
    first_slot = jax.random.randint(pick_key, (), 0, half_count).astype(jnp.int32)
    second_slot = first_slot + half_count
    first_value = order[first_slot]
    wanted = jnp.where(first_value == TILES - 1, first_value - 1, first_value + 1).astype(jnp.int32)
    where_wanted = jnp.argmax((order == wanted).astype(jnp.int32)).astype(jnp.int32)
    second_value = order[second_slot]
    order = order.at[where_wanted].set(second_value)
    order = order.at[second_slot].set(wanted)
    return order


def touch_ends(drawn, own_key, smallest, high):
    place = [jax.random.randint(jax.random.fold_in(own_key, axis), (), 0, length) for axis, length in enumerate(drawn.shape)]
    widest = drawn.shape.index(max(drawn.shape))
    neighbour = place[:widest] + [(place[widest] + 1) % drawn.shape[widest]] + place[widest + 1:]
    return drawn.at[tuple(place)].set(smallest).at[tuple(neighbour)].set(high)


def block_levels(own_key, extent, split, smallest, largest):
    level, own = 1.0, jax.random.fold_in(own_key, 6)
    for position, shards_of in split:
        heights = jnp.exp(jax.random.uniform(jax.random.fold_in(own, position), (shards_of,), jnp.float32, smallest / len(split), largest / len(split)))
        level = level * jnp.repeat(heights, extent[position] // shards_of).reshape([-1 if axis == position else 1 for axis in range(len(extent))])
    return level


def noise(key, extent, deviation, reach, cuts=(), kind=jnp.bfloat16):
    entries = deviation * jax.random.normal(key, extent, jnp.float32)
    if cuts:
        entries = entries * block_levels(key, extent, cuts, -0.22, 0.18)
    return jnp.clip(entries, -reach, reach).astype(kind)


def setup_inputs(seed: int = 0) -> dict:
    splits = jax.random.split(jax.random.key(seed), 7)
    mask_tiles = noise(splits[0], (TILES, TILE_PX, TILE_PX), 1.0, 6.0, ((0, 16),))
    slot_pos = draw_slot_pos(jax.random.fold_in(splits[6], 71), 0)
    src_shift = touch_ends(jax.random.randint(splits[2], (SOURCES, 2), 0 - SHIFT_MAX, SHIFT_MAX + 1), jax.random.fold_in(splits[2], 1), 0 - SHIFT_MAX, SHIFT_MAX).astype(jnp.int32)
    src_weight = touch_ends(jax.random.randint(splits[3], (SOURCES,), 1, 9), jax.random.fold_in(splits[3], 1), 1, 8).astype(jnp.int32)
    pupil_phase = jnp.clip(jax.random.uniform(splits[4], (FREQ, FREQ), jnp.float32, -3.140625, 3.140625), -3.140625, 3.140625)
    target = jnp.clip(1.0 * jax.random.uniform(splits[5], (TILES, TILE_PX, TILE_PX), jnp.float32) ** block_levels(splits[5], (TILES, TILE_PX, TILE_PX), ((0, 16),), -0.2, 0.2), 0.0, 1.0).astype(jnp.bfloat16)
    return dict(mask_tiles=mask_tiles, slot_pos=slot_pos, src_shift=src_shift, src_weight=src_weight, pupil_phase=pupil_phase, target=target)


steepness = 4.0
threshold = 0.6
learn_rate = 8.0

def hdot(left, right):
    return jnp.dot(left, right, precision=lax.Precision.HIGHEST, preferred_element_type=jnp.float32)

def angle_table(positions, frequency, period):
    wrapped = jnp.mod(positions[:, None] * frequency[None, :], period)
    return wrapped.astype(jnp.float32) * (2.0 * math.pi / period)

def pupil_parts(shift_pair, pupil_phase, frequency):
    padded = jnp.pad(pupil_phase, FREQ)
    shift_a = shift_pair[0].astype(jnp.int32)
    shift_b = shift_pair[1].astype(jnp.int32)
    window = lax.dynamic_slice(padded, (FREQ + shift_a, FREQ + shift_b), (FREQ, FREQ))
    along_bins = frequency + shift_a
    across = frequency + shift_b
    inside = along_bins[:, None] * along_bins[:, None] + across[None, :] * across[None, :] <= PUPIL_R * PUPIL_R
    return (jnp.where(inside, jnp.cos(window), 0.0), jnp.where(inside, jnp.sin(window), 0.0))

def reference(mask_tiles, slot_pos, src_shift, src_weight, pupil_phase, target):
    frequency = jnp.arange(FREQ, dtype=jnp.int32) - FREQ // 2
    col_angles = angle_table(jnp.arange(TILE_PX, dtype=jnp.int32), frequency, TILE_PX)
    col_cos = jnp.cos(col_angles)
    col_sin = jnp.sin(col_angles)
    col_cos_b = col_cos.astype(jnp.bfloat16)
    col_sin_b = col_sin.astype(jnp.bfloat16)
    col_both = jnp.concatenate([col_cos_b, col_sin_b], axis=1)
    col_cos_bt = col_cos_b.astype(jnp.float32).T
    col_sin_bt = col_sin_b.astype(jnp.float32).T
    row_angles = angle_table(jnp.arange(EXT_PX, dtype=jnp.int32), frequency, EXT_PX)
    row_cos = jnp.cos(row_angles)
    row_sin = jnp.sin(row_angles)
    out_angles = angle_table(jnp.arange(TILE_PX, dtype=jnp.int32) + HALO, frequency, EXT_PX)
    out_table = jnp.concatenate([jnp.cos(out_angles), jnp.sin(out_angles)], axis=1).astype(jnp.bfloat16)
    scale_factor = 1.0 / (FREQ / 2 * math.sqrt(EXT_PX * TILE_PX))
    holder = jnp.zeros((TILES,), jnp.int32).at[slot_pos].set(jnp.arange(TILES, dtype=jnp.int32))
    clip_mask = mask_tiles[holder]
    clip_target = target[holder]
    rim_zeros = jnp.zeros((1, HALO, TILE_PX), jnp.bfloat16)
    upper_rim = jnp.concatenate([rim_zeros, clip_mask[:-1, TILE_PX - HALO:]], axis=0)
    lower_rim = jnp.concatenate([clip_mask[1:, :HALO], rim_zeros], axis=0)
    patches = jnp.concatenate([upper_rim, clip_mask, lower_rim], axis=1)
    pupils_re, pupils_im = jax.vmap(lambda pair: pupil_parts(pair, pupil_phase, frequency))(src_shift)
    weights = src_weight.astype(jnp.float32) / (4.0 * SOURCES)

    def tile_work(inputs):
        tile_patch, tile_target = inputs
        half_spec = jnp.dot(tile_patch, col_both, preferred_element_type=jnp.float32)
        half_re = half_spec[:, :FREQ]
        half_im = -half_spec[:, FREQ:]
        spec_re = hdot(row_cos.T, half_re) + hdot(row_sin.T, half_im)
        spec_im = hdot(row_cos.T, half_im) - hdot(row_sin.T, half_re)

        def make_stack(pupil_re, pupil_im):
            amp_re = scale_factor * (pupil_re * spec_re - pupil_im * spec_im)
            amp_im = scale_factor * (pupil_re * spec_im + pupil_im * spec_re)
            line_re = (hdot(amp_re, col_cos.T) - hdot(amp_im, col_sin.T)).astype(jnp.bfloat16)
            line_im = (hdot(amp_re, col_sin.T) + hdot(amp_im, col_cos.T)).astype(jnp.bfloat16)
            top_half = jnp.concatenate([line_re, line_im], axis=1)
            low_half = jnp.concatenate([-line_im, line_re], axis=1)
            return jnp.concatenate([top_half, low_half], axis=0)
        stacks = jax.vmap(make_stack)(pupils_re, pupils_im)

        def add_image(total_image, inputs):
            line_stack, weight = inputs
            field_rows = jnp.dot(out_table, line_stack, preferred_element_type=jnp.float32)
            squared = field_rows * field_rows
            return (total_image + weight * (squared[:, :TILE_PX] + squared[:, TILE_PX:]), None)
        intensity = lax.scan(add_image, jnp.zeros((TILE_PX, TILE_PX), jnp.float32), (stacks, weights))[0]
        resist_tile = jax.nn.sigmoid(steepness * (intensity - threshold))
        adjoint = (2.0 * (resist_tile - tile_target.astype(jnp.float32)) * steepness * resist_tile * (1.0 - resist_tile)).astype(jnp.bfloat16)
        adjoint_wide = jnp.concatenate([adjoint, adjoint], axis=1).astype(jnp.float32)

        def add_grad(totals, inputs):
            line_stack, weight, pupil_re, pupil_im = inputs
            field_rows = jnp.dot(out_table, line_stack, preferred_element_type=jnp.float32)
            dfield = (2.0 * weight * adjoint_wide * field_rows).astype(jnp.bfloat16)
            blocks = lax.dot_general(out_table, dfield, (((0,), (0,)), ((), ())), preferred_element_type=jnp.float32)
            dline_re = blocks[:FREQ, :TILE_PX] + blocks[FREQ:, TILE_PX:]
            dline_im = blocks[:FREQ, TILE_PX:] - blocks[FREQ:, :TILE_PX]
            damp_re = hdot(dline_re, col_cos) + hdot(dline_im, col_sin)
            damp_im = hdot(dline_im, col_cos) - hdot(dline_re, col_sin)
            grad_re = totals[0] + scale_factor * (pupil_re * damp_re + pupil_im * damp_im)
            grad_im = totals[1] + scale_factor * (pupil_re * damp_im - pupil_im * damp_re)
            return ((grad_re, grad_im), None)
        empty = jnp.zeros((FREQ, FREQ), jnp.float32)
        grads = lax.scan(add_grad, (empty, empty), (stacks, weights, pupils_re, pupils_im))[0]
        return (resist_tile, grads[0], grads[1])
    resist_clip, grads_re, grads_im = lax.map(tile_work, (patches, clip_target))

    def patch_gradient(inputs):
        grad_re, grad_im = inputs
        back_re = hdot(row_cos, grad_re) - hdot(row_sin, grad_im)
        back_im = hdot(row_sin, grad_re) + hdot(row_cos, grad_im)
        return hdot(back_re, col_cos_bt) - hdot(back_im, col_sin_bt)
    patch_grads = lax.map(patch_gradient, (grads_re, grads_im))
    zero_rows = jnp.zeros((1, HALO, TILE_PX), jnp.float32)
    inner_rows = patch_grads[:, HALO:HALO + TILE_PX]
    from_above = jnp.concatenate([zero_rows, patch_grads[:-1, TILE_PX + HALO:]], axis=0)
    from_below = jnp.concatenate([patch_grads[1:, :HALO], zero_rows], axis=0)
    step_clip = inner_rows.at[:, :HALO].add(from_above).at[:, TILE_PX - HALO:].add(from_below)
    return (resist_clip[slot_pos], -learn_rate * step_clip[slot_pos])
```

```python
import functools
import math

import jax
import jax.numpy as jnp
import numpy as np
from jax import lax
from jax.experimental import pallas as pl
from jax.experimental.pallas import tpu as pltpu
from jax.sharding import PartitionSpec as P

TILE_PX = 1024
HALO = 64
FREQ = 128
PUPIL_R = 28
SRC_DEV = 2
EXT_PX = 1152
MESH = pl.DeviceIdType.MESH
HIGH = lax.Precision.HIGH
HIGHEST = lax.Precision.HIGHEST

steepness = 4.0
threshold = 0.6
learn_rate = 8.0


def np_tables(positions, period):
    frequency = np.arange(FREQ, dtype=np.int64) - FREQ // 2
    wrapped = np.mod(positions[:, None] * frequency[None, :], period).astype(np.float64)
    angles = wrapped * (2.0 * math.pi / period)
    return np.cos(angles).astype(np.float32), np.sin(angles).astype(np.float32)


def fdot(left, right, precision):
    return jnp.dot(left, right, precision=precision, preferred_element_type=jnp.float32)


def group_sizes(tile_count):
    low = 4 if tile_count % 4 == 0 else 1
    return low, tile_count // low


def greet(tile_count):
    low, high = group_sizes(tile_count)
    tile = lax.axis_index("tile")
    src = lax.axis_index("src")
    my_high, my_low = tile // low, tile % low
    barrier = pltpu.get_barrier_semaphore()
    for k in range(1, high):
        peer = ((my_high + k) % high) * low + my_low
        pl.semaphore_signal(barrier, inc=1, device_id={"tile": peer}, device_id_type=MESH)
    for j in range(1, low):
        peer = my_high * low + (my_low + j) % low
        pl.semaphore_signal(barrier, inc=1, device_id={"tile": peer}, device_id_type=MESH)
    src_count = lax.axis_size("src")
    for k in range(1, src_count):
        peer = (src + k) % src_count
        pl.semaphore_signal(barrier, inc=1, device_id={"src": peer}, device_id_type=MESH)
    pl.semaphore_wait(barrier, high - 1 + low - 1 + src_count - 1)


def start_high(tile_count, held, sends, recvs):
    low, high = group_sizes(tile_count)
    tile = lax.axis_index("tile")
    my_high, my_low = tile // low, tile % low
    copies = []
    for k in range(1, high):
        peer = ((my_high + k) % high) * low + my_low
        copy = pltpu.make_async_remote_copy(
            src_ref=held.at[my_low, my_high],
            dst_ref=held.at[my_low, my_high],
            send_sem=sends.at[k - 1],
            recv_sem=recvs.at[k - 1],
            device_id={"tile": peer},
            device_id_type=MESH,
        )
        copy.start()
        copies.append(copy)
    return copies


def start_low(tile_count, held, sends, recvs):
    low, high = group_sizes(tile_count)
    tile = lax.axis_index("tile")
    my_high, my_low = tile // low, tile % low
    copies = []
    for j in range(1, low):
        peer = my_high * low + (my_low + j) % low
        copy = pltpu.make_async_remote_copy(
            src_ref=held.at[my_low],
            dst_ref=held.at[my_low],
            send_sem=sends.at[j - 1],
            recv_sem=recvs.at[j - 1],
            device_id={"tile": peer},
            device_id_type=MESH,
        )
        copy.start()
        copies.append(copy)
    return copies


def pick(tile_count, held, pick_ref):
    low, high = group_sizes(tile_count)
    block = held[pick_ref[0], pick_ref[1]].astype(jnp.float32)
    return jnp.where(pick_ref[2] > 0, block, 0.0)


def start_src(held, sends, recvs):
    src = lax.axis_index("src")
    src_count = lax.axis_size("src")
    copies = []
    for k in range(1, src_count):
        copy = pltpu.make_async_remote_copy(
            src_ref=held.at[src],
            dst_ref=held.at[src],
            send_sem=sends.at[k - 1],
            recv_sem=recvs.at[k - 1],
            device_id={"src": (src + k) % src_count},
            device_id_type=MESH,
        )
        copy.start()
        copies.append(copy)
    return copies


def rim_kernel(
    tile_count, pick_ref, rim_ref, meta_ref, rims_out, meta_out,
    held, rims, meta_held, send_a, recv_a, send_b, recv_b, send_s, recv_s, send_r, recv_r
):
    low, high = group_sizes(tile_count)
    tile = lax.axis_index("tile")
    src = lax.axis_index("src")
    side = src % 2
    held[tile % low, tile // low] = rim_ref[...]
    meta_held[src] = meta_ref[...]
    greet(tile_count)
    meta_copies = start_src(meta_held, send_s, recv_s)
    for copy in start_high(tile_count, held, send_a, recv_a):
        copy.wait()
    for copy in start_low(tile_count, held, send_b, recv_b):
        copy.wait()
    rims[side] = pick(tile_count, held, pick_ref).astype(jnp.bfloat16)
    rim_copy = pltpu.make_async_remote_copy(
        src_ref=rims.at[side],
        dst_ref=rims.at[side],
        send_sem=send_r.at[0],
        recv_sem=recv_r.at[0],
        device_id={"src": src + 1 - 2 * side},
        device_id_type=MESH,
    )
    rim_copy.start()
    for copy in meta_copies:
        copy.wait()
    meta_out[...] = meta_held[...]
    rim_copy.wait()
    rims_out[...] = rims[...]


def back_kernel(
    tile_count, pick_ref, grad_ref, rim_table, own_table, out_ref,
    held, grads, total, send_a, recv_a, send_b, recv_b, send_s, recv_s
):
    low, high = group_sizes(tile_count)
    tile = lax.axis_index("tile")
    src = lax.axis_index("src")
    src_count = lax.axis_size("src")
    grads[src] = grad_ref[...]
    greet(tile_count)
    for copy in start_src(grads, send_s, recv_s):
        copy.wait()
    both = grads[0]
    for k in range(1, src_count):
        both = both + grads[k]
    total[:FREQ, :] = both
    total[FREQ:, :FREQ] = -both[:, FREQ:]
    total[FREQ:, FREQ:] = both[:, :FREQ]
    rim_back = fdot(rim_table[...], total[...], HIGHEST)
    held[tile % low, tile // low] = rim_back.astype(jnp.bfloat16)
    high_copies = start_high(tile_count, held, send_a, recv_a)
    out_ref[...] = fdot(own_table[...], total[...], HIGHEST)
    for copy in high_copies:
        copy.wait()
    for copy in start_low(tile_count, held, send_b, recv_b):
        copy.wait()
    block = pick(tile_count, held, pick_ref)
    rows = out_ref.shape[0]
    first = jnp.where(src == 0, 1.0, 0.0)
    last = jnp.where(src == src_count - 1, 1.0, 0.0)
    out_ref[:HALO, :] += first * block
    out_ref[rows - HALO :, :] += last * block


def comm_scratch(tile_count):
    low, high = group_sizes(tile_count)
    dma = pltpu.SemaphoreType.DMA
    sems = [dma((max(high - 1, 1),))] * 2 + [dma((max(low - 1, 1),))] * 2 + [dma((max(lax.axis_size("src") - 1, 1),))] * 2
    held = pltpu.VMEM((low, high, HALO, 2 * FREQ), jnp.bfloat16)
    return held, sems


def exchange_rims(tile_count, choice, rim, meta):
    held, sems = comm_scratch(tile_count)
    block = (HALO, 2 * FREQ)
    metas = (lax.axis_size("src"), *meta.shape)
    vmem = pl.BlockSpec(memory_space=pltpu.VMEM)
    return pl.pallas_call(
        functools.partial(rim_kernel, tile_count),
        out_shape=[
            jax.ShapeDtypeStruct((2, *block), jnp.bfloat16),
            jax.ShapeDtypeStruct(metas, jnp.int32),
        ],
        in_specs=[pl.BlockSpec(memory_space=pltpu.SMEM), vmem, vmem],
        out_specs=[vmem] * 2,
        scratch_shapes=[
            held,
            pltpu.VMEM((2, *block), jnp.bfloat16),
            pltpu.VMEM(metas, jnp.int32),
            *sems,
            pltpu.SemaphoreType.DMA((1,)),
            pltpu.SemaphoreType.DMA((1,)),
        ],
        compiler_params=pltpu.CompilerParams(
            collective_id=0, has_side_effects=True, vmem_limit_bytes=16 * 2**20
        ),
        cost_estimate=pl.CostEstimate(flops=0, bytes_accessed=2**20, transcendentals=0),
    )(choice, rim, meta)


def exchange_back(tile_count, choice, grad, rim_table, own_table):
    held, sems = comm_scratch(tile_count)
    vmem = pl.BlockSpec(memory_space=pltpu.VMEM)
    return pl.pallas_call(
        functools.partial(back_kernel, tile_count),
        out_shape=jax.ShapeDtypeStruct(own_table.shape, jnp.float32),
        in_specs=[pl.BlockSpec(memory_space=pltpu.SMEM), vmem, vmem, vmem],
        out_specs=vmem,
        scratch_shapes=[
            held,
            pltpu.VMEM((lax.axis_size("src"), *grad.shape), jnp.float32),
            pltpu.VMEM((2 * FREQ, 2 * FREQ), jnp.float32),
            *sems,
        ],
        compiler_params=pltpu.CompilerParams(
            collective_id=1, has_side_effects=True, vmem_limit_bytes=16 * 2**20
        ),
        cost_estimate=pl.CostEstimate(flops=10**8, bytes_accessed=2**21, transcendentals=0),
    )(choice, grad, rim_table, own_table)


def pupil_parts(shift_pair, pupil_phase, frequency):
    padded = jnp.pad(pupil_phase, FREQ)
    shift_a = shift_pair[0]
    shift_b = shift_pair[1]
    window = lax.dynamic_slice(padded, (FREQ + shift_a, FREQ + shift_b), (FREQ, FREQ))
    along_bins = frequency + shift_a
    across = frequency + shift_b
    inside = (
        along_bins[:, None] * along_bins[:, None] + across[None, :] * across[None, :]
        <= PUPIL_R * PUPIL_R
    )
    return (jnp.where(inside, jnp.cos(window), 0.0), jnp.where(inside, jnp.sin(window), 0.0))


def per_device(mask_tiles, slot_pos, src_shift, src_weight, pupil_phase, target):
    tile_count = lax.axis_size("tile")
    src_count = lax.axis_size("src")
    my_slot = lax.axis_index("tile")
    my_src = lax.axis_index("src")
    row_share = TILE_PX // src_count
    sources_total = SRC_DEV * src_count
    frequency = jnp.arange(FREQ, dtype=jnp.int32) - FREQ // 2
    col_cos, col_sin = np_tables(np.arange(TILE_PX), TILE_PX)
    row_cos, row_sin = np_tables(np.arange(EXT_PX), EXT_PX)
    col_both = np.concatenate([col_cos, col_sin], axis=1).astype(jnp.bfloat16)
    last_table = np.concatenate([col_cos.T, -col_sin.T], axis=0).astype(jnp.bfloat16)
    line_table = np.block([[col_cos.T, col_sin.T], [-col_sin.T, col_cos.T]])
    damp_table = np.ascontiguousarray(line_table.T)
    row_both = np.concatenate([row_cos, row_sin], axis=1)
    out_table = row_both[HALO : HALO + TILE_PX].astype(jnp.bfloat16)
    scale_factor = 1.0 / (FREQ / 2 * math.sqrt(EXT_PX * TILE_PX))

    slot_ids = jnp.arange(tile_count, dtype=jnp.int32)
    my_position = jnp.sum(jnp.where(slot_ids == my_slot, slot_pos, 0))
    wanted = jnp.where(my_src % 2 == 0, my_position - 1, my_position + 1)
    there = slot_pos == wanted
    wanted_slot = jnp.sum(jnp.where(there, slot_ids, 0))
    low, _ = group_sizes(tile_count)
    choice = jnp.stack(
        [wanted_slot % low, wanted_slot // low, jnp.any(there).astype(jnp.int32)]
    ).astype(jnp.int32)

    own_tile = mask_tiles[0]
    half_own = jnp.dot(own_tile, col_both, preferred_element_type=jnp.float32)
    my_rim = jnp.where(my_src % 2 == 0, half_own[TILE_PX - HALO :], half_own[:HALO])
    meta = jnp.concatenate([src_shift, src_weight[:, None]], axis=1)
    meta_block = jnp.pad(meta, ((0, 8 - SRC_DEV), (0, 128 - 3)))
    rims, metas = exchange_rims(tile_count, choice, my_rim.astype(jnp.bfloat16), meta_block)
    rims = rims.astype(jnp.float32)
    half_all = jnp.concatenate([rims[0], half_own, rims[1]], axis=0)
    meta_all = metas[:, :SRC_DEV, :3].reshape(sources_total, 3)

    spec4 = fdot(row_both.T, half_all, HIGH)
    spec_re = spec4[:FREQ, :FREQ] - spec4[FREQ:, FREQ:]
    spec_im = -spec4[:FREQ, FREQ:] - spec4[FREQ:, :FREQ]
    weights = meta_all[:, 2].astype(jnp.float32) / (4.0 * sources_total)
    pupils = [pupil_parts(meta_all[s], pupil_phase, frequency) for s in range(sources_total)]
    amps = jnp.concatenate(
        [
            jnp.concatenate(
                [
                    scale_factor * (pupil_re * spec_re - pupil_im * spec_im),
                    scale_factor * (pupil_re * spec_im + pupil_im * spec_re),
                ],
                axis=1,
            )
            for pupil_re, pupil_im in pupils
        ],
        axis=0,
    )
    lines = fdot(amps, line_table, HIGH).astype(jnp.bfloat16)

    my_table = lax.dynamic_slice_in_dim(jnp.asarray(out_table), my_src * row_share, row_share, 0)
    kept_fields = []
    intensity = jnp.zeros((row_share, TILE_PX), jnp.float32)
    for s in range(sources_total):
        top = lines[s * FREQ : (s + 1) * FREQ]
        swapped = jnp.concatenate([-top[:, TILE_PX:], top[:, :TILE_PX]], axis=1)
        stack = jnp.concatenate([top, swapped], axis=0)
        fields = jnp.dot(my_table, stack, preferred_element_type=jnp.float32)
        squared = fields * fields
        intensity = intensity + weights[s] * (squared[:, :TILE_PX] + squared[:, TILE_PX:])
        kept_fields.append(fields)
    my_target = lax.dynamic_slice_in_dim(target[0], my_src * row_share, row_share, 0).astype(
        jnp.float32
    )
    resist_rows = jax.nn.sigmoid(steepness * (intensity - threshold))
    adjoint = (
        2.0 * (resist_rows - my_target) * steepness * resist_rows * (1.0 - resist_rows)
    ).astype(jnp.bfloat16)
    adjoint_wide = jnp.concatenate([adjoint, adjoint], axis=1).astype(jnp.float32)
    dlines = []
    for s in range(sources_total):
        dfield = (2.0 * weights[s] * adjoint_wide * kept_fields[s]).astype(jnp.bfloat16)
        blocks = lax.dot_general(
            my_table, dfield, (((0,), (0,)), ((), ())), preferred_element_type=jnp.float32
        )
        dline_re = blocks[:FREQ, :TILE_PX] + blocks[FREQ:, TILE_PX:]
        dline_im = blocks[:FREQ, TILE_PX:] - blocks[FREQ:, :TILE_PX]
        dlines.append(jnp.concatenate([dline_re, dline_im], axis=1))
    damps = fdot(jnp.concatenate(dlines, axis=0), damp_table, HIGH)
    grad_re = jnp.zeros((FREQ, FREQ), jnp.float32)
    grad_im = jnp.zeros((FREQ, FREQ), jnp.float32)
    for s, (pupil_re, pupil_im) in enumerate(pupils):
        damp_re = damps[s * FREQ : (s + 1) * FREQ, :FREQ]
        damp_im = damps[s * FREQ : (s + 1) * FREQ, FREQ:]
        grad_re = grad_re + scale_factor * (pupil_re * damp_re + pupil_im * damp_im)
        grad_im = grad_im + scale_factor * (pupil_re * damp_im - pupil_im * damp_re)
    grad = jnp.concatenate([grad_re, grad_im], axis=1)

    row_array = jnp.asarray(row_both)
    own_table = lax.dynamic_slice_in_dim(row_array, HALO + my_src * row_share, row_share, 0)
    rim_start = jnp.where(my_src % 2 == 0, EXT_PX - HALO, 0)
    rim_table = lax.dynamic_slice_in_dim(row_array, rim_start, HALO, 0)
    back_rows = exchange_back(tile_count, choice, grad, rim_table, own_table)
    step_rows = jnp.dot(
        back_rows.astype(jnp.bfloat16), last_table, preferred_element_type=jnp.float32
    )
    return (resist_rows[None], (-learn_rate * step_rows)[None])


def solution(mesh):
    return jax.shard_map(
        per_device,
        mesh=mesh,
        in_specs=(P("tile", None, None), P(), P("src", None), P("src"), P(), P("tile", None, None)),
        out_specs=(P("tile", "src", None), P("tile", "src", None)),
        check_vma=False,
    )
```

```python
import functools
import math

import jax
import jax.numpy as jnp
import numpy as np
from jax import lax
from jax.experimental import pallas as pl
from jax.experimental.pallas import tpu as pltpu
from jax.sharding import PartitionSpec as P

TILE_PX = 1024
HALO = 64
FREQ = 128
PUPIL_R = 28
SRC_DEV = 2
EXT_PX = 1152
MESH = pl.DeviceIdType.MESH
HIGHEST = lax.Precision.HIGHEST

steepness = 4.0
threshold = 0.6
learn_rate = 8.0


def np_tables(positions, period):
    frequency = np.arange(FREQ, dtype=np.int64) - FREQ // 2
    wrapped = np.mod(positions[:, None] * frequency[None, :], period).astype(np.float64)
    angles = wrapped * (2.0 * math.pi / period)
    return np.cos(angles).astype(np.float32), np.sin(angles).astype(np.float32)


def fdot(left, right, precision):
    return jnp.dot(left, right, precision=precision, preferred_element_type=jnp.float32)


def group_sizes(tile_count):
    low = 4 if tile_count % 4 == 0 else 1
    return low, tile_count // low


def greet(tile_count):
    low, high = group_sizes(tile_count)
    tile = lax.axis_index("tile")
    src = lax.axis_index("src")
    my_high, my_low = tile // low, tile % low
    barrier = pltpu.get_barrier_semaphore()
    src_count = lax.axis_size("src")
    for k in range(1, high):
        peer = ((my_high + k) % high) * low + my_low
        pl.semaphore_signal(barrier, inc=1, device_id={"tile": peer}, device_id_type=MESH)
    for j in range(1, low):
        peer = my_high * low + (my_low + j) % low
        pl.semaphore_signal(barrier, inc=1, device_id={"tile": peer}, device_id_type=MESH)
    for k in range(1, src_count):
        peer = (src + k) % src_count
        pl.semaphore_signal(barrier, inc=1, device_id={"src": peer}, device_id_type=MESH)
    pl.semaphore_wait(barrier, high - 1 + low - 1 + src_count - 1)


def start_high(tile_count, held, sends, recvs):
    low, high = group_sizes(tile_count)
    tile = lax.axis_index("tile")
    my_high, my_low = tile // low, tile % low
    copies = []
    for k in range(1, high):
        peer = ((my_high + k) % high) * low + my_low
        copy = pltpu.make_async_remote_copy(
            src_ref=held.at[my_low, my_high],
            dst_ref=held.at[my_low, my_high],
            send_sem=sends.at[k - 1],
            recv_sem=recvs.at[k - 1],
            device_id={"tile": peer},
            device_id_type=MESH,
        )
        copy.start()
        copies.append(copy)
    return copies


def start_low(tile_count, held, sends, recvs):
    low, high = group_sizes(tile_count)
    tile = lax.axis_index("tile")
    my_high, my_low = tile // low, tile % low
    copies = []
    for j in range(1, low):
        peer = my_high * low + (my_low + j) % low
        copy = pltpu.make_async_remote_copy(
            src_ref=held.at[my_low],
            dst_ref=held.at[my_low],
            send_sem=sends.at[j - 1],
            recv_sem=recvs.at[j - 1],
            device_id={"tile": peer},
            device_id_type=MESH,
        )
        copy.start()
        copies.append(copy)
    return copies


def pick(tile_count, held, pos_ref):
    low, _ = group_sizes(tile_count)
    side = lax.axis_index("src") % 2
    wanted = pos_ref[lax.axis_index("tile")] - 1 + 2 * side
    slot = jnp.int32(0)
    found = jnp.int32(0)
    for i in range(tile_count):
        hit = pos_ref[i] == wanted
        slot = slot + jnp.where(hit, i, 0)
        found = found + jnp.where(hit, 1, 0)
    block = held[slot % low, slot // low].astype(jnp.float32)
    return jnp.where(found > 0, block, 0.0)


def start_src(held, sends, recvs):
    src = lax.axis_index("src")
    src_count = lax.axis_size("src")
    copies = []
    for k in range(1, src_count):
        copy = pltpu.make_async_remote_copy(
            src_ref=held.at[src],
            dst_ref=held.at[src],
            send_sem=sends.at[k - 1],
            recv_sem=recvs.at[k - 1],
            device_id={"src": (src + k) % src_count},
            device_id_type=MESH,
        )
        copy.start()
        copies.append(copy)
    return copies


def rim_kernel(
    tile_count, pos_ref, shift_ref, weight_ref, mask_ref, table_ref, rims_out, meta_out, half_out,
    held, rims, meta_held, send_a, recv_a, send_b, recv_b, send_s, recv_s, send_r, recv_r
):
    low, high = group_sizes(tile_count)
    tile = lax.axis_index("tile")
    src = lax.axis_index("src")
    side = src % 2
    row = lax.broadcasted_iota(jnp.int32, (8, 128), 0)
    col = lax.broadcasted_iota(jnp.int32, (8, 128), 1)
    meta = jnp.zeros((8, 128), jnp.int32)
    for p in range(SRC_DEV):
        meta = jnp.where((row == p) & (col == 0), shift_ref[p, 0], meta)
        meta = jnp.where((row == p) & (col == 1), shift_ref[p, 1], meta)
        meta = jnp.where((row == p) & (col == 2), weight_ref[p], meta)
    meta_held[src] = meta
    start = pl.multiple_of((1 - side) * (TILE_PX - HALO), HALO)
    rim = jnp.dot(
        mask_ref[0, pl.ds(start, HALO), :], table_ref[...], preferred_element_type=jnp.float32
    )
    held[tile % low, tile // low] = rim.astype(jnp.bfloat16)
    greet(tile_count)
    high_copies = start_high(tile_count, held, send_a, recv_a)
    meta_copies = start_src(meta_held, send_s, recv_s)
    for copy in high_copies:
        copy.wait()
    low_copies = start_low(tile_count, held, send_b, recv_b)

    def transform(i, carry):
        at = pl.ds(pl.multiple_of(i * 256, 256), 256)
        half_out[at, :] = jnp.dot(
            mask_ref[0, at, :], table_ref[...], preferred_element_type=jnp.float32
        )
        return carry

    lax.fori_loop(0, TILE_PX // 256, transform, 0)
    for copy in low_copies:
        copy.wait()
    rims[side] = pick(tile_count, held, pos_ref).astype(jnp.bfloat16)
    rim_copy = pltpu.make_async_remote_copy(
        src_ref=rims.at[side],
        dst_ref=rims.at[side],
        send_sem=send_r.at[0],
        recv_sem=recv_r.at[0],
        device_id={"src": src + 1 - 2 * side},
        device_id_type=MESH,
    )
    rim_copy.start()
    for copy in meta_copies:
        copy.wait()
    meta_out[...] = meta_held[...]
    rim_copy.wait()
    rims_out[...] = rims[...]


def back_kernel(
    tile_count, pos_ref, grad_ref, rim_table, own_table, out_ref,
    held, grads, total, send_a, recv_a, send_b, recv_b, send_s, recv_s
):
    low, high = group_sizes(tile_count)
    tile = lax.axis_index("tile")
    src = lax.axis_index("src")
    src_count = lax.axis_size("src")
    grads[src] = grad_ref[...]
    greet(tile_count)
    for copy in start_src(grads, send_s, recv_s):
        copy.wait()
    both = grads[0]
    for k in range(1, src_count):
        both = both + grads[k]
    total[:FREQ, :] = both
    total[FREQ:, :FREQ] = -both[:, FREQ:]
    total[FREQ:, FREQ:] = both[:, :FREQ]
    rim_back = fdot(rim_table[...], total[...], HIGHEST)
    held[tile % low, tile // low] = rim_back.astype(jnp.bfloat16)
    high_copies = start_high(tile_count, held, send_a, recv_a)
    out_ref[...] = fdot(own_table[...], total[...], HIGHEST)
    for copy in high_copies:
        copy.wait()
    for copy in start_low(tile_count, held, send_b, recv_b):
        copy.wait()
    block = pick(tile_count, held, pos_ref)
    rows = out_ref.shape[0]
    first = jnp.where(src == 0, 1.0, 0.0)
    last = jnp.where(src == src_count - 1, 1.0, 0.0)
    out_ref[:HALO, :] += first * block
    out_ref[rows - HALO :, :] += last * block


def comm_scratch(tile_count):
    low, high = group_sizes(tile_count)
    dma = pltpu.SemaphoreType.DMA
    sems = [dma((max(high - 1, 1),))] * 2 + [dma((max(low - 1, 1),))] * 2 + [dma((max(lax.axis_size("src") - 1, 1),))] * 2
    held = pltpu.VMEM((low, high, HALO, 2 * FREQ), jnp.bfloat16)
    return held, sems


def exchange_rims(tile_count, slot_pos, src_shift, src_weight, mask_tiles, table):
    held, sems = comm_scratch(tile_count)
    block = (HALO, 2 * FREQ)
    metas = (lax.axis_size("src"), 8, 128)
    vmem = pl.BlockSpec(memory_space=pltpu.VMEM)
    smem = pl.BlockSpec(memory_space=pltpu.SMEM)
    return pl.pallas_call(
        functools.partial(rim_kernel, tile_count),
        out_shape=[
            jax.ShapeDtypeStruct((2, *block), jnp.bfloat16),
            jax.ShapeDtypeStruct(metas, jnp.int32),
            jax.ShapeDtypeStruct((TILE_PX, 2 * FREQ), jnp.float32),
        ],
        in_specs=[smem, smem, smem, vmem, vmem],
        out_specs=[vmem] * 3,
        scratch_shapes=[
            held,
            pltpu.VMEM((2, *block), jnp.bfloat16),
            pltpu.VMEM(metas, jnp.int32),
            *sems,
            pltpu.SemaphoreType.DMA((1,)),
            pltpu.SemaphoreType.DMA((1,)),
        ],
        compiler_params=pltpu.CompilerParams(
            collective_id=0, has_side_effects=True, vmem_limit_bytes=24 * 2**20
        ),
        cost_estimate=pl.CostEstimate(flops=6 * 10**8, bytes_accessed=2**22, transcendentals=0),
    )(slot_pos, src_shift, src_weight, mask_tiles, table)


def split(value):
    top = value.astype(jnp.bfloat16)
    return top, (value - top.astype(jnp.float32)).astype(jnp.bfloat16)


def np_split(value):
    top = value.astype(jnp.bfloat16)
    return top, (value - top.astype(np.float32)).astype(jnp.bfloat16)


def bdot(left, right):
    return jnp.dot(left, right, preferred_element_type=jnp.float32)


def bdot_t(left, right):
    return lax.dot_general(
        left, right, (((1,), (1,)), ((), ())), preferred_element_type=jnp.float32
    )


def image_kernel(
    sources_total, scale_factor, place_ref, meta_ref,
    half_ref, rims_ref, own_top, own_low, rim_top, rim_low, phase_ref, line_top, line_low,
    table_ref, table_t_ref, target_ref, resist_ref, grad_ref,
    pupil_re, pupil_im, amp_top, amp_low, fields, damps, dlines
):
    step = pl.program_id(0)
    width = target_ref.shape[2]

    @pl.when(step == 0)
    def _():
        half_top, half_low = split(half_ref[...])
        spec4 = bdot(own_top[...], half_top)
        spec4 += bdot(own_top[...], half_low) + bdot(own_low[...], half_top)
        rims = rims_ref[...].reshape(2 * HALO, 2 * FREQ)
        spec4 += bdot(rim_top[...], rims) + bdot(rim_low[...], rims)
        spec_re = scale_factor * (spec4[:FREQ, :FREQ] - spec4[FREQ:, FREQ:])
        spec_im = -scale_factor * (spec4[:FREQ, FREQ:] + spec4[FREQ:, :FREQ])
        f_a = lax.broadcasted_iota(jnp.int32, (FREQ, FREQ), 0) - FREQ // 2
        f_b = lax.broadcasted_iota(jnp.int32, (FREQ, FREQ), 1) - FREQ // 2
        inside = f_a * f_a + f_b * f_b <= PUPIL_R * PUPIL_R
        phase_re = jnp.where(inside, jnp.cos(phase_ref[...]), 0.0)
        phase_im = jnp.where(inside, jnp.sin(phase_ref[...]), 0.0)
        for s in range(sources_total):
            move_a = (FREQ - meta_ref[s // SRC_DEV, s % SRC_DEV, 0]) % FREQ
            move_b = (FREQ - meta_ref[s // SRC_DEV, s % SRC_DEV, 1]) % FREQ
            p_re = pltpu.roll(pltpu.roll(phase_re, move_a, 0), move_b, 1)
            p_im = pltpu.roll(pltpu.roll(phase_im, move_a, 0), move_b, 1)
            pupil_re[s] = p_re
            pupil_im[s] = p_im
            at = slice(s * FREQ, (s + 1) * FREQ)
            for part, value in (
                (slice(0, FREQ), p_re * spec_re - p_im * spec_im),
                (slice(FREQ, 2 * FREQ), p_re * spec_im + p_im * spec_re),
            ):
                top, low = split(value)
                amp_top[at, part] = top
                amp_low[at, part] = low
        damps[...] = jnp.zeros_like(damps)

    table = table_ref[...]
    intensity = jnp.zeros((table.shape[0], width), jnp.float32)
    weights = []
    for s in range(sources_total):
        weight = meta_ref[s // SRC_DEV, s % SRC_DEV, 2].astype(jnp.float32)
        weight = weight * (1.0 / (4.0 * sources_total))
        weights.append(weight)
        at = slice(s * FREQ, (s + 1) * FREQ)
        line = bdot(amp_top[at, :], line_top[...])
        line += bdot(amp_top[at, :], line_low[...]) + bdot(amp_low[at, :], line_top[...])
        re, im = line[:, :width].astype(jnp.bfloat16), line[:, width:].astype(jnp.bfloat16)
        field_re = bdot(table, jnp.concatenate([re, -im], axis=0))
        field_im = bdot(table, jnp.concatenate([im, re], axis=0))
        fields[s, :, :width] = field_re
        fields[s, :, width:] = field_im
        intensity += weight * (field_re * field_re + field_im * field_im)
    resist = 1.0 / (1.0 + jnp.exp(-steepness * (intensity - threshold)))
    resist_ref[0] = resist
    adjoint = 2.0 * (resist - target_ref[0].astype(jnp.float32)) * steepness
    adjoint = (adjoint * resist * (1.0 - resist)).astype(jnp.bfloat16).astype(jnp.float32)
    for s in range(sources_total):
        factor = 2.0 * weights[s] * adjoint
        d_re = (factor * fields[s, :, :width]).astype(jnp.bfloat16)
        d_im = (factor * fields[s, :, width:]).astype(jnp.bfloat16)
        b_re = bdot(table_t_ref[...], d_re)
        b_im = bdot(table_t_ref[...], d_im)
        at = slice(s * FREQ, (s + 1) * FREQ)
        dlines[at, :width] = b_re[:FREQ] + b_im[FREQ:]
        dlines[at, width:] = b_im[:FREQ] - b_re[FREQ:]
    d_top, d_low = split(dlines[...])
    damps[...] += (
        bdot_t(d_top, line_top[...]) + bdot_t(d_top, line_low[...]) + bdot_t(d_low, line_top[...])
    )

    @pl.when(step == pl.num_programs(0) - 1)
    def _():
        grad_re = jnp.zeros((FREQ, FREQ), jnp.float32)
        grad_im = jnp.zeros((FREQ, FREQ), jnp.float32)
        for s in range(sources_total):
            at = slice(s * FREQ, (s + 1) * FREQ)
            damp_re, damp_im = damps[at, :FREQ], damps[at, FREQ:]
            grad_re += pupil_re[s] * damp_re + pupil_im[s] * damp_im
            grad_im += pupil_re[s] * damp_im - pupil_im[s] * damp_re
        grad_ref[:, :FREQ] = scale_factor * grad_re
        grad_ref[:, FREQ:] = scale_factor * grad_im


def image_step(place, metas, half, rims, row_tables, phase, lines, table, table_t, target, rows):
    sources_total = SRC_DEV * metas.shape[0]
    scale_factor = 1.0 / (FREQ / 2 * math.sqrt(EXT_PX * TILE_PX))
    width = 256
    wide = 2 * FREQ

    def whole(*shape):
        return pl.BlockSpec(shape, lambda j, place, meta: (0,) * len(shape))

    grid_spec = pltpu.PrefetchScalarGridSpec(
        num_scalar_prefetch=2,
        grid=(TILE_PX // width,),
        in_specs=[
            whole(TILE_PX, wide),
            whole(2, HALO, wide),
            whole(wide, TILE_PX),
            whole(wide, TILE_PX),
            whole(wide, 2 * HALO),
            whole(wide, 2 * HALO),
            whole(FREQ, FREQ),
            pl.BlockSpec((wide, 2 * width), lambda j, place, meta: (0, j)),
            pl.BlockSpec((wide, 2 * width), lambda j, place, meta: (0, j)),
            pl.BlockSpec((rows, wide), lambda j, place, meta: (place[0], 0)),
            pl.BlockSpec((wide, rows), lambda j, place, meta: (0, place[0])),
            pl.BlockSpec((1, rows, width), lambda j, place, meta: (0, place[0], j)),
        ],
        out_specs=[
            pl.BlockSpec((1, rows, width), lambda j, place, meta: (0, 0, j)),
            whole(FREQ, wide),
        ],
        scratch_shapes=[
            pltpu.VMEM((sources_total, FREQ, FREQ), jnp.float32),
            pltpu.VMEM((sources_total, FREQ, FREQ), jnp.float32),
            pltpu.VMEM((sources_total * FREQ, wide), jnp.bfloat16),
            pltpu.VMEM((sources_total * FREQ, wide), jnp.bfloat16),
            pltpu.VMEM((sources_total, rows, 2 * width), jnp.float32),
            pltpu.VMEM((sources_total * FREQ, wide), jnp.float32),
            pltpu.VMEM((sources_total * FREQ, 2 * width), jnp.float32),
        ],
    )
    return pl.pallas_call(
        functools.partial(image_kernel, sources_total, scale_factor),
        grid_spec=grid_spec,
        out_shape=[
            jax.ShapeDtypeStruct((1, rows, TILE_PX), jnp.float32),
            jax.ShapeDtypeStruct((FREQ, wide), jnp.float32),
        ],
        compiler_params=pltpu.CompilerParams(vmem_limit_bytes=48 * 2**20),
        cost_estimate=pl.CostEstimate(flops=10**10, bytes_accessed=10**7, transcendentals=10**6),
    )(place, metas, half, rims, *row_tables, phase, *lines, table, table_t, target)


def exchange_back(tile_count, choice, grad, rim_table, own_table):
    held, sems = comm_scratch(tile_count)
    vmem = pl.BlockSpec(memory_space=pltpu.VMEM)
    return pl.pallas_call(
        functools.partial(back_kernel, tile_count),
        out_shape=jax.ShapeDtypeStruct(own_table.shape, jnp.float32),
        in_specs=[pl.BlockSpec(memory_space=pltpu.SMEM), vmem, vmem, vmem],
        out_specs=vmem,
        scratch_shapes=[
            held,
            pltpu.VMEM((lax.axis_size("src"), *grad.shape), jnp.float32),
            pltpu.VMEM((2 * FREQ, 2 * FREQ), jnp.float32),
            *sems,
        ],
        compiler_params=pltpu.CompilerParams(
            collective_id=1, has_side_effects=True, vmem_limit_bytes=16 * 2**20
        ),
        cost_estimate=pl.CostEstimate(flops=10**8, bytes_accessed=2**21, transcendentals=0),
    )(choice, grad, rim_table, own_table)


def per_device(mask_tiles, slot_pos, src_shift, src_weight, pupil_phase, target):
    tile_count = lax.axis_size("tile")
    my_src = lax.axis_index("src")
    rows = TILE_PX // lax.axis_size("src")
    col_cos, col_sin = np_tables(np.arange(TILE_PX), TILE_PX)
    row_cos, row_sin = np_tables(np.arange(EXT_PX), EXT_PX)
    col_both = np.concatenate([col_cos, col_sin], axis=1).astype(jnp.bfloat16)
    last_table = np.concatenate([col_cos.T, -col_sin.T], axis=0).astype(jnp.bfloat16)
    line_table = np.stack(
        [
            np.concatenate([col_cos.T, -col_sin.T], axis=0).reshape(2 * FREQ, -1, 256),
            np.concatenate([col_sin.T, col_cos.T], axis=0).reshape(2 * FREQ, -1, 256),
        ],
        axis=2,
    ).reshape(2 * FREQ, 2 * TILE_PX)
    row_both = np.concatenate([row_cos, row_sin], axis=1)
    row_own = np.ascontiguousarray(row_both[HALO : HALO + TILE_PX].T)
    row_rim = np.concatenate([row_both[:HALO], row_both[EXT_PX - HALO :]], axis=0).T
    row_tables = (*np_split(row_own), *np_split(np.ascontiguousarray(row_rim)))
    out_table = row_both[HALO : HALO + TILE_PX].astype(jnp.bfloat16)

    rims, metas, half_own = exchange_rims(
        tile_count, slot_pos, src_shift, src_weight, mask_tiles, col_both
    )
    place = jnp.full((1,), my_src, jnp.int32)
    resist, grad = image_step(
        place, metas, half_own, rims, row_tables, pupil_phase, np_split(line_table),
        out_table, np.ascontiguousarray(out_table.T), target, rows
    )
    row_array = jnp.asarray(row_both)
    own_table = lax.dynamic_slice_in_dim(row_array, HALO + my_src * rows, rows, 0)
    rim_start = jnp.where(my_src % 2 == 0, EXT_PX - HALO, 0)
    rim_table = lax.dynamic_slice_in_dim(row_array, rim_start, HALO, 0)
    back_rows = exchange_back(tile_count, slot_pos, grad, rim_table, own_table)
    step_rows = jnp.dot(
        back_rows.astype(jnp.bfloat16), last_table, preferred_element_type=jnp.float32
    )
    return (resist, (-learn_rate * step_rows)[None])


def solution(mesh):
    return jax.shard_map(
        per_device,
        mesh=mesh,
        in_specs=(P("tile", None, None), P(), P("src", None), P("src"), P(), P("tile", None, None)),
        out_specs=(P("tile", "src", None), P("tile", "src", None)),
        check_vma=False,
    )
```

```python
import functools
import math

import jax
import jax.numpy as jnp
import numpy as np
from jax import lax
from jax.experimental import pallas as pl
from jax.experimental.pallas import tpu as pltpu
from jax.sharding import PartitionSpec as P

TILE_PX = 1024
HALO = 64
FREQ = 128
PUPIL_R = 28
SRC_DEV = 2
EXT_PX = 1152
MESH = pl.DeviceIdType.MESH
HIGHEST = lax.Precision.HIGHEST

steepness = 4.0
threshold = 0.6
learn_rate = 8.0


def np_tables(positions, period):
    frequency = np.arange(FREQ, dtype=np.int64) - FREQ // 2
    wrapped = np.mod(positions[:, None] * frequency[None, :], period).astype(np.float64)
    angles = wrapped * (2.0 * math.pi / period)
    return np.cos(angles).astype(np.float32), np.sin(angles).astype(np.float32)


def fdot(left, right, precision):
    return jnp.dot(left, right, precision=precision, preferred_element_type=jnp.float32)


def group_sizes(tile_count):
    low = 4 if tile_count % 4 == 0 else 1
    return low, tile_count // low


def low_peers(low, my_low):
    if low == 1:
        return []
    return [(my_low + 2) % 4, my_low + 1 - 2 * (my_low % 2)]


def greet(tile_count):
    low, high = group_sizes(tile_count)
    tile = lax.axis_index("tile")
    src = lax.axis_index("src")
    my_high, my_low = tile // low, tile % low
    barrier = pltpu.get_barrier_semaphore()
    src_count = lax.axis_size("src")
    for k in range(1, high):
        peer = ((my_high + k) % high) * low + my_low
        pl.semaphore_signal(barrier, inc=1, device_id={"tile": peer}, device_id_type=MESH)
    near = low_peers(low, my_low)
    for other in near:
        peer = my_high * low + other
        pl.semaphore_signal(barrier, inc=1, device_id={"tile": peer}, device_id_type=MESH)
    for k in range(1, src_count):
        peer = (src + k) % src_count
        pl.semaphore_signal(barrier, inc=1, device_id={"src": peer}, device_id_type=MESH)
    pl.semaphore_wait(barrier, high - 1 + len(near) + src_count - 1)


def start_high(tile_count, held, sends, recvs):
    low, high = group_sizes(tile_count)
    tile = lax.axis_index("tile")
    my_high, my_low = tile // low, tile % low
    copies = []
    for k in range(1, high):
        peer = ((my_high + k) % high) * low + my_low
        copy = pltpu.make_async_remote_copy(
            src_ref=held.at[my_low, my_high],
            dst_ref=held.at[my_low, my_high],
            send_sem=sends.at[k - 1],
            recv_sem=recvs.at[k - 1],
            device_id={"tile": peer},
            device_id_type=MESH,
        )
        copy.start()
        copies.append(copy)
    return copies


def start_low(tile_count, held, sends, recvs):
    low, high = group_sizes(tile_count)
    tile = lax.axis_index("tile")
    my_high, my_low = tile // low, tile % low

    def copy_of(which, block, other):
        return pltpu.make_async_remote_copy(
            src_ref=held.at[block],
            dst_ref=held.at[block],
            send_sem=sends.at[which],
            recv_sem=recvs.at[which],
            device_id={"tile": my_high * low + other},
            device_id_type=MESH,
        )

    if low == 1:
        return lambda: None
    far, beside = low_peers(low, my_low)
    first = copy_of(0, my_low, far)
    first.start()
    second = copy_of(1, my_low, beside)
    second.start()

    def finish():
        first.wait()
        third = copy_of(2, far, beside)
        third.start()
        second.wait()
        third.wait()

    return finish


def pick(tile_count, held, pos_ref):
    low, _ = group_sizes(tile_count)
    side = lax.axis_index("src") % 2
    wanted = pos_ref[lax.axis_index("tile")] - 1 + 2 * side
    slot = jnp.int32(0)
    found = jnp.int32(0)
    for i in range(tile_count):
        hit = pos_ref[i] == wanted
        slot = slot + jnp.where(hit, i, 0)
        found = found + jnp.where(hit, 1, 0)
    block = held[slot % low, slot // low].astype(jnp.float32)
    return jnp.where(found > 0, block, 0.0)


def start_src(held, sends, recvs):
    src = lax.axis_index("src")
    src_count = lax.axis_size("src")
    copies = []
    for k in range(1, src_count):
        copy = pltpu.make_async_remote_copy(
            src_ref=held.at[src],
            dst_ref=held.at[src],
            send_sem=sends.at[k - 1],
            recv_sem=recvs.at[k - 1],
            device_id={"src": (src + k) % src_count},
            device_id_type=MESH,
        )
        copy.start()
        copies.append(copy)
    return copies


def rim_kernel(
    tile_count, pos_ref, shift_ref, weight_ref, mask_ref, table_ref, own_top, own_low, phase_ref,
    rims_out, meta_out, spec_out, pupil_out, held, rims, meta_held, send_a, recv_a, send_b, recv_b, send_s, recv_s, send_r, recv_r
):
    low, high = group_sizes(tile_count)
    tile = lax.axis_index("tile")
    src = lax.axis_index("src")
    side = src % 2
    row = lax.broadcasted_iota(jnp.int32, (8, 128), 0)
    col = lax.broadcasted_iota(jnp.int32, (8, 128), 1)
    meta = jnp.zeros((8, 128), jnp.int32)
    for p in range(SRC_DEV):
        meta = jnp.where((row == p) & (col == 0), shift_ref[p, 0], meta)
        meta = jnp.where((row == p) & (col == 1), shift_ref[p, 1], meta)
        meta = jnp.where((row == p) & (col == 2), weight_ref[p], meta)
    meta_held[src] = meta
    start = pl.multiple_of((1 - side) * (TILE_PX - HALO), HALO)
    rim = jnp.dot(
        mask_ref[0, pl.ds(start, HALO), :], table_ref[...], preferred_element_type=jnp.float32
    )
    held[tile % low, tile // low] = rim.astype(jnp.bfloat16)
    greet(tile_count)
    high_copies = start_high(tile_count, held, send_a, recv_a)
    meta_copies = start_src(meta_held, send_s, recv_s)
    for copy in high_copies:
        copy.wait()
    finish_low = start_low(tile_count, held, send_b, recv_b)
    spec = jnp.zeros((2 * FREQ, 2 * FREQ), jnp.float32)
    for i in range(TILE_PX // 256):
        at = slice(i * 256, (i + 1) * 256)
        half_top, half_low = split(bdot(mask_ref[0, at, :], table_ref[...]))
        spec += bdot(own_top[:, at], half_top)
        spec += bdot(own_top[:, at], half_low) + bdot(own_low[:, at], half_top)
    spec_out[...] = spec
    finish_low()
    rims[side] = pick(tile_count, held, pos_ref).astype(jnp.bfloat16)
    rim_copy = pltpu.make_async_remote_copy(
        src_ref=rims.at[side],
        dst_ref=rims.at[side],
        send_sem=send_r.at[0],
        recv_sem=recv_r.at[0],
        device_id={"src": src + 1 - 2 * side},
        device_id_type=MESH,
    )
    rim_copy.start()
    f_a = lax.broadcasted_iota(jnp.int32, (FREQ, FREQ), 0) - FREQ // 2
    f_b = lax.broadcasted_iota(jnp.int32, (FREQ, FREQ), 1) - FREQ // 2
    inside = f_a * f_a + f_b * f_b <= PUPIL_R * PUPIL_R
    pupil_out[0] = jnp.where(inside, jnp.cos(phase_ref[...]), 0.0)
    pupil_out[1] = jnp.where(inside, jnp.sin(phase_ref[...]), 0.0)
    for copy in meta_copies:
        copy.wait()
    meta_out[...] = meta_held[...]
    rim_copy.wait()
    rims_out[...] = rims[...]


def back_kernel(
    tile_count, pos_ref, grad_ref, row_table, out_ref,
    held, grads, total, send_a, recv_a, send_b, recv_b, send_s, recv_s
):
    low, high = group_sizes(tile_count)
    tile = lax.axis_index("tile")
    src = lax.axis_index("src")
    src_count = lax.axis_size("src")
    grads[src] = grad_ref[...]
    greet(tile_count)
    for copy in start_src(grads, send_s, recv_s):
        copy.wait()
    both = grads[0]
    for k in range(1, src_count):
        both = both + grads[k]
    total[:FREQ, :] = both
    total[FREQ:, :FREQ] = -both[:, FREQ:]
    total[FREQ:, FREQ:] = both[:, :FREQ]
    rim_at = pl.multiple_of((1 - src % 2) * (EXT_PX - HALO), HALO)
    rim_back = fdot(row_table[pl.ds(rim_at, HALO), :], total[...], HIGHEST)
    held[tile % low, tile // low] = rim_back.astype(jnp.bfloat16)
    high_copies = start_high(tile_count, held, send_a, recv_a)
    rows = out_ref.shape[0]
    own_at = pl.multiple_of(HALO + src * rows, HALO)
    out_ref[...] = fdot(row_table[pl.ds(own_at, rows), :], total[...], HIGHEST)
    for copy in high_copies:
        copy.wait()
    start_low(tile_count, held, send_b, recv_b)()
    block = pick(tile_count, held, pos_ref)
    first = jnp.where(src == 0, 1.0, 0.0)
    last = jnp.where(src == src_count - 1, 1.0, 0.0)
    out_ref[:HALO, :] += first * block
    out_ref[rows - HALO :, :] += last * block


def comm_scratch(tile_count):
    low, high = group_sizes(tile_count)
    dma = pltpu.SemaphoreType.DMA
    sems = [dma((max(high - 1, 1),))] * 2 + [dma((max(low - 1, 1),))] * 2 + [dma((max(lax.axis_size("src") - 1, 1),))] * 2
    held = pltpu.VMEM((low, high, HALO, 2 * FREQ), jnp.bfloat16)
    return held, sems


def exchange_rims(tile_count, slot_pos, src_shift, src_weight, mask_tiles, *tables):
    held, sems = comm_scratch(tile_count)
    block = (HALO, 2 * FREQ)
    metas = (lax.axis_size("src"), 8, 128)
    vmem = pl.BlockSpec(memory_space=pltpu.VMEM)
    smem = pl.BlockSpec(memory_space=pltpu.SMEM)
    return pl.pallas_call(
        functools.partial(rim_kernel, tile_count),
        out_shape=[
            jax.ShapeDtypeStruct((2, *block), jnp.bfloat16),
            jax.ShapeDtypeStruct(metas, jnp.int32),
            jax.ShapeDtypeStruct((2 * FREQ, 2 * FREQ), jnp.float32),
            jax.ShapeDtypeStruct((2, FREQ, FREQ), jnp.float32),
        ],
        in_specs=[smem, smem, smem, vmem] + [vmem] * len(tables),
        out_specs=[vmem] * 4,
        scratch_shapes=[
            held,
            pltpu.VMEM((2, *block), jnp.bfloat16),
            pltpu.VMEM(metas, jnp.int32),
            *sems,
            pltpu.SemaphoreType.DMA((1,)),
            pltpu.SemaphoreType.DMA((1,)),
        ],
        compiler_params=pltpu.CompilerParams(
            collective_id=0, has_side_effects=True, vmem_limit_bytes=56 * 2**20
        ),
        cost_estimate=pl.CostEstimate(flops=6 * 10**8, bytes_accessed=2**22, transcendentals=0),
    )(slot_pos, src_shift, src_weight, mask_tiles, *tables)


def split(value):
    top = value.astype(jnp.bfloat16)
    return top, (value - top.astype(jnp.float32)).astype(jnp.bfloat16)


def np_split(value):
    top = value.astype(jnp.bfloat16)
    return top, (value - top.astype(np.float32)).astype(jnp.bfloat16)


def bdot(left, right):
    return jnp.dot(left, right, preferred_element_type=jnp.float32)


def bdot_t(left, right):
    return lax.dot_general(
        left, right, (((1,), (1,)), ((), ())), preferred_element_type=jnp.float32
    )


def image_kernel(
    sources_total, scale_factor, place_ref, meta_ref,
    spec_ref, rims_ref, rim_top, rim_low, phase_ref, line_top, line_low,
    table_ref, table_t_ref, target_ref, resist_ref, grad_ref,
    pupil_re, pupil_im, amp_top, amp_low, fields, damps, dlines
):
    step = pl.program_id(0)
    width = target_ref.shape[2]

    @pl.when(step == 0)
    def _():
        rims = rims_ref[...].reshape(2 * HALO, 2 * FREQ)
        spec4 = spec_ref[...] + bdot(rim_top[...], rims) + bdot(rim_low[...], rims)
        spec_re = scale_factor * (spec4[:FREQ, :FREQ] - spec4[FREQ:, FREQ:])
        spec_im = -scale_factor * (spec4[:FREQ, FREQ:] + spec4[FREQ:, :FREQ])
        phase_re, phase_im = phase_ref[0], phase_ref[1]
        for s in range(sources_total):
            move_a = (FREQ - meta_ref[s // SRC_DEV, s % SRC_DEV, 0]) % FREQ
            move_b = (FREQ - meta_ref[s // SRC_DEV, s % SRC_DEV, 1]) % FREQ
            p_re = pltpu.roll(pltpu.roll(phase_re, move_a, 0), move_b, 1)
            p_im = pltpu.roll(pltpu.roll(phase_im, move_a, 0), move_b, 1)
            pupil_re[s] = p_re
            pupil_im[s] = p_im
            at = slice(s * FREQ, (s + 1) * FREQ)
            for part, value in (
                (slice(0, FREQ), p_re * spec_re - p_im * spec_im),
                (slice(FREQ, 2 * FREQ), p_re * spec_im + p_im * spec_re),
            ):
                top, low = split(value)
                amp_top[at, part] = top
                amp_low[at, part] = low
        damps[...] = jnp.zeros_like(damps)

    table = table_ref[...]
    intensity = jnp.zeros((table.shape[0], width), jnp.float32)
    weights = []
    for s in range(sources_total):
        weight = meta_ref[s // SRC_DEV, s % SRC_DEV, 2].astype(jnp.float32)
        weight = weight * (1.0 / (4.0 * sources_total))
        weights.append(weight)
        at = slice(s * FREQ, (s + 1) * FREQ)
        line = bdot(amp_top[at, :], line_top[...])
        line += bdot(amp_top[at, :], line_low[...]) + bdot(amp_low[at, :], line_top[...])
        re, im = line[:, :width].astype(jnp.bfloat16), line[:, width:].astype(jnp.bfloat16)
        field_re = bdot(table, jnp.concatenate([re, -im], axis=0))
        field_im = bdot(table, jnp.concatenate([im, re], axis=0))
        fields[s, :, :width] = field_re
        fields[s, :, width:] = field_im
        intensity += weight * (field_re * field_re + field_im * field_im)
    resist = 1.0 / (1.0 + jnp.exp(-steepness * (intensity - threshold)))
    resist_ref[0] = resist
    adjoint = 2.0 * (resist - target_ref[0].astype(jnp.float32)) * steepness
    adjoint = (adjoint * resist * (1.0 - resist)).astype(jnp.bfloat16).astype(jnp.float32)
    for s in range(sources_total):
        factor = 2.0 * weights[s] * adjoint
        d_re = (factor * fields[s, :, :width]).astype(jnp.bfloat16)
        d_im = (factor * fields[s, :, width:]).astype(jnp.bfloat16)
        b_re = bdot(table_t_ref[...], d_re)
        b_im = bdot(table_t_ref[...], d_im)
        at = slice(s * FREQ, (s + 1) * FREQ)
        dlines[at, :width] = (b_re[:FREQ] + b_im[FREQ:]).astype(jnp.bfloat16)
        dlines[at, width:] = (b_im[:FREQ] - b_re[FREQ:]).astype(jnp.bfloat16)
    damps[...] += bdot_t(dlines[...], line_top[...])

    @pl.when(step == pl.num_programs(0) - 1)
    def _():
        grad_re = jnp.zeros((FREQ, FREQ), jnp.float32)
        grad_im = jnp.zeros((FREQ, FREQ), jnp.float32)
        for s in range(sources_total):
            at = slice(s * FREQ, (s + 1) * FREQ)
            damp_re, damp_im = damps[at, :FREQ], damps[at, FREQ:]
            grad_re += pupil_re[s] * damp_re + pupil_im[s] * damp_im
            grad_im += pupil_re[s] * damp_im - pupil_im[s] * damp_re
        grad_ref[:, :FREQ] = scale_factor * grad_re
        grad_ref[:, FREQ:] = scale_factor * grad_im


def image_step(place, metas, spec, rims, row_tables, phase, lines, table, table_t, target, rows):
    sources_total = SRC_DEV * metas.shape[0]
    scale_factor = 1.0 / (FREQ / 2 * math.sqrt(EXT_PX * TILE_PX))
    width = 256
    wide = 2 * FREQ

    def whole(*shape):
        return pl.BlockSpec(shape, lambda j, place, meta: (0,) * len(shape))

    grid_spec = pltpu.PrefetchScalarGridSpec(
        num_scalar_prefetch=2,
        grid=(TILE_PX // width,),
        in_specs=[
            whole(wide, wide),
            whole(2, HALO, wide),
            whole(wide, 2 * HALO),
            whole(wide, 2 * HALO),
            whole(2, FREQ, FREQ),
            pl.BlockSpec((wide, 2 * width), lambda j, place, meta: (0, j)),
            pl.BlockSpec((wide, 2 * width), lambda j, place, meta: (0, j)),
            pl.BlockSpec((rows, wide), lambda j, place, meta: (place[0], 0)),
            pl.BlockSpec((wide, rows), lambda j, place, meta: (0, place[0])),
            pl.BlockSpec((1, rows, width), lambda j, place, meta: (0, place[0], j)),
        ],
        out_specs=[
            pl.BlockSpec((1, rows, width), lambda j, place, meta: (0, 0, j)),
            whole(FREQ, wide),
        ],
        scratch_shapes=[
            pltpu.VMEM((sources_total, FREQ, FREQ), jnp.float32),
            pltpu.VMEM((sources_total, FREQ, FREQ), jnp.float32),
            pltpu.VMEM((sources_total * FREQ, wide), jnp.bfloat16),
            pltpu.VMEM((sources_total * FREQ, wide), jnp.bfloat16),
            pltpu.VMEM((sources_total, rows, 2 * width), jnp.float32),
            pltpu.VMEM((sources_total * FREQ, wide), jnp.float32),
            pltpu.VMEM((sources_total * FREQ, 2 * width), jnp.bfloat16),
        ],
    )
    return pl.pallas_call(
        functools.partial(image_kernel, sources_total, scale_factor),
        grid_spec=grid_spec,
        out_shape=[
            jax.ShapeDtypeStruct((1, rows, TILE_PX), jnp.float32),
            jax.ShapeDtypeStruct((FREQ, wide), jnp.float32),
        ],
        compiler_params=pltpu.CompilerParams(vmem_limit_bytes=48 * 2**20),
        cost_estimate=pl.CostEstimate(flops=10**10, bytes_accessed=10**7, transcendentals=10**6),
    )(place, metas, spec, rims, *row_tables, phase, *lines, table, table_t, target)


def exchange_back(tile_count, slot_pos, grad, row_table, rows):
    held, sems = comm_scratch(tile_count)
    vmem = pl.BlockSpec(memory_space=pltpu.VMEM)
    return pl.pallas_call(
        functools.partial(back_kernel, tile_count),
        out_shape=jax.ShapeDtypeStruct((rows, 2 * FREQ), jnp.float32),
        in_specs=[pl.BlockSpec(memory_space=pltpu.SMEM), vmem, vmem],
        out_specs=vmem,
        scratch_shapes=[
            held,
            pltpu.VMEM((lax.axis_size("src"), *grad.shape), jnp.float32),
            pltpu.VMEM((2 * FREQ, 2 * FREQ), jnp.float32),
            *sems,
        ],
        compiler_params=pltpu.CompilerParams(
            collective_id=1, has_side_effects=True, vmem_limit_bytes=56 * 2**20
        ),
        cost_estimate=pl.CostEstimate(flops=10**8, bytes_accessed=2**21, transcendentals=0),
    )(slot_pos, grad, row_table)


def per_device(mask_tiles, slot_pos, src_shift, src_weight, pupil_phase, target):
    tile_count = lax.axis_size("tile")
    my_src = lax.axis_index("src")
    rows = TILE_PX // lax.axis_size("src")
    col_cos, col_sin = np_tables(np.arange(TILE_PX), TILE_PX)
    row_cos, row_sin = np_tables(np.arange(EXT_PX), EXT_PX)
    col_both = np.concatenate([col_cos, col_sin], axis=1).astype(jnp.bfloat16)
    last_table = np.concatenate([col_cos.T, -col_sin.T], axis=0).astype(jnp.bfloat16)
    line_table = np.stack(
        [
            np.concatenate([col_cos.T, -col_sin.T], axis=0).reshape(2 * FREQ, -1, 256),
            np.concatenate([col_sin.T, col_cos.T], axis=0).reshape(2 * FREQ, -1, 256),
        ],
        axis=2,
    ).reshape(2 * FREQ, 2 * TILE_PX)
    row_both = np.concatenate([row_cos, row_sin], axis=1)
    row_own = np.ascontiguousarray(row_both[HALO : HALO + TILE_PX].T)
    row_rim = np.concatenate([row_both[:HALO], row_both[EXT_PX - HALO :]], axis=0).T
    rim_tables = np_split(np.ascontiguousarray(row_rim))
    out_table = row_both[HALO : HALO + TILE_PX].astype(jnp.bfloat16)

    rims, metas, spec_own, pupil = exchange_rims(
        tile_count, slot_pos, src_shift, src_weight, mask_tiles, col_both,
        *np_split(row_own), pupil_phase
    )
    place = jnp.full((1,), my_src, jnp.int32)
    resist, grad = image_step(
        place, metas, spec_own, rims, rim_tables, pupil, np_split(line_table),
        out_table, np.ascontiguousarray(out_table.T), target, rows
    )
    back_rows = exchange_back(tile_count, slot_pos, grad, row_both, rows)
    step_rows = jnp.dot(
        back_rows.astype(jnp.bfloat16), last_table, preferred_element_type=jnp.float32
    )
    return (resist, (-learn_rate * step_rows)[None])


def solution(mesh):
    return jax.shard_map(
        per_device,
        mesh=mesh,
        in_specs=(P("tile", None, None), P(), P("src", None), P("src"), P(), P("tile", None, None)),
        out_specs=(P("tile", "src", None), P("tile", "src", None)),
        check_vma=False,
    )
```

```python
import functools
import math

import jax
import jax.numpy as jnp
import numpy as np
from jax import lax
from jax.experimental import pallas as pl
from jax.experimental.pallas import tpu as pltpu
from jax.sharding import PartitionSpec as P

TILE_PX = 1024
HALO = 64
FREQ = 128
PUPIL_R = 28
SRC_DEV = 2
EXT_PX = 1152
MESH = pl.DeviceIdType.MESH
HIGHEST = lax.Precision.HIGHEST

steepness = 4.0
threshold = 0.6
learn_rate = 8.0


def np_tables(positions, period):
    frequency = np.arange(FREQ, dtype=np.int64) - FREQ // 2
    wrapped = np.mod(positions[:, None] * frequency[None, :], period).astype(np.float64)
    angles = wrapped * (2.0 * math.pi / period)
    return np.cos(angles).astype(np.float32), np.sin(angles).astype(np.float32)


def fdot(left, right, precision):
    return jnp.dot(left, right, precision=precision, preferred_element_type=jnp.float32)


def group_sizes(tile_count):
    low = 4 if tile_count % 4 == 0 else 1
    return low, tile_count // low


def low_peers(low, my_low):
    if low == 1:
        return []
    return [(my_low + 2) % 4, my_low + 1 - 2 * (my_low % 2)]


def greet(tile_count):
    low, high = group_sizes(tile_count)
    tile = lax.axis_index("tile")
    src = lax.axis_index("src")
    my_high, my_low = tile // low, tile % low
    barrier = pltpu.get_barrier_semaphore()
    src_count = lax.axis_size("src")
    for k in range(1, high):
        peer = ((my_high + k) % high) * low + my_low
        pl.semaphore_signal(barrier, inc=1, device_id={"tile": peer}, device_id_type=MESH)
    near = low_peers(low, my_low)
    for other in near:
        peer = my_high * low + other
        pl.semaphore_signal(barrier, inc=1, device_id={"tile": peer}, device_id_type=MESH)
    for k in range(1, src_count):
        peer = (src + k) % src_count
        pl.semaphore_signal(barrier, inc=1, device_id={"src": peer}, device_id_type=MESH)
    pl.semaphore_wait(barrier, high - 1 + len(near) + src_count - 1)


def start_high(tile_count, held, sends, recvs):
    low, high = group_sizes(tile_count)
    tile = lax.axis_index("tile")
    my_high, my_low = tile // low, tile % low
    copies = []
    for k in range(1, high):
        peer = ((my_high + k) % high) * low + my_low
        copy = pltpu.make_async_remote_copy(
            src_ref=held.at[my_low, my_high],
            dst_ref=held.at[my_low, my_high],
            send_sem=sends.at[k - 1],
            recv_sem=recvs.at[k - 1],
            device_id={"tile": peer},
            device_id_type=MESH,
        )
        copy.start()
        copies.append(copy)
    return copies


def start_low(tile_count, held, sends, recvs):
    low, high = group_sizes(tile_count)
    tile = lax.axis_index("tile")
    my_high, my_low = tile // low, tile % low

    def copy_of(which, block, other):
        return pltpu.make_async_remote_copy(
            src_ref=held.at[block],
            dst_ref=held.at[block],
            send_sem=sends.at[which],
            recv_sem=recvs.at[which],
            device_id={"tile": my_high * low + other},
            device_id_type=MESH,
        )

    if low == 1:
        return lambda: None
    far, beside = low_peers(low, my_low)
    first = copy_of(0, my_low, far)
    first.start()
    second = copy_of(1, my_low, beside)
    second.start()

    def finish():
        first.wait()
        third = copy_of(2, far, beside)
        third.start()
        second.wait()
        third.wait()

    return finish


def pick(tile_count, held, pos_ref):
    low, _ = group_sizes(tile_count)
    side = lax.axis_index("src") % 2
    wanted = pos_ref[lax.axis_index("tile")] - 1 + 2 * side
    slot = jnp.int32(0)
    found = jnp.int32(0)
    for i in range(tile_count):
        hit = pos_ref[i] == wanted
        slot = slot + jnp.where(hit, i, 0)
        found = found + jnp.where(hit, 1, 0)
    block = held[slot % low, slot // low].astype(jnp.float32)
    return jnp.where(found > 0, block, 0.0)


def start_src(held, sends, recvs):
    src = lax.axis_index("src")
    src_count = lax.axis_size("src")
    copies = []
    for k in range(1, src_count):
        copy = pltpu.make_async_remote_copy(
            src_ref=held.at[src],
            dst_ref=held.at[src],
            send_sem=sends.at[k - 1],
            recv_sem=recvs.at[k - 1],
            device_id={"src": (src + k) % src_count},
            device_id_type=MESH,
        )
        copy.start()
        copies.append(copy)
    return copies


def rim_kernel(
    tile_count, pos_ref, shift_ref, weight_ref, mask_hbm, table_ref, top_hbm, low_hbm, phase_ref,
    rims_out, meta_out, spec_out, pupil_out, held, rims, meta_held, send_a, recv_a, send_b, recv_b, send_s, recv_s, send_r, recv_r,
    rim_ref, mask_ref, own_top, own_low, load
):
    low, high = group_sizes(tile_count)
    tile = lax.axis_index("tile")
    src = lax.axis_index("src")
    side = src % 2
    start = pl.multiple_of((1 - side) * (TILE_PX - HALO), HALO)
    rim_load = pltpu.make_async_copy(mask_hbm.at[0, pl.ds(start, HALO), :], rim_ref, load.at[0])
    rim_load.start()
    loads = [
        pltpu.make_async_copy(mask_hbm.at[0], mask_ref, load.at[1]),
        pltpu.make_async_copy(top_hbm, own_top, load.at[2]),
        pltpu.make_async_copy(low_hbm, own_low, load.at[3]),
    ]
    for copy in loads:
        copy.start()
    row = lax.broadcasted_iota(jnp.int32, (8, 128), 0)
    col = lax.broadcasted_iota(jnp.int32, (8, 128), 1)
    meta = jnp.zeros((8, 128), jnp.int32)
    for p in range(SRC_DEV):
        meta = jnp.where((row == p) & (col == 0), shift_ref[p, 0], meta)
        meta = jnp.where((row == p) & (col == 1), shift_ref[p, 1], meta)
        meta = jnp.where((row == p) & (col == 2), weight_ref[p], meta)
    meta_held[src] = meta
    rim_load.wait()
    rim = bdot(rim_ref[...], table_ref[...])
    held[tile % low, tile // low] = rim.astype(jnp.bfloat16)
    greet(tile_count)
    high_copies = start_high(tile_count, held, send_a, recv_a)
    meta_copies = start_src(meta_held, send_s, recv_s)
    for copy in high_copies:
        copy.wait()
    finish_low = start_low(tile_count, held, send_b, recv_b)
    for copy in loads:
        copy.wait()
    spec = jnp.zeros((2 * FREQ, 2 * FREQ), jnp.float32)
    for i in range(TILE_PX // 256):
        at = slice(i * 256, (i + 1) * 256)
        half_top, half_low = split(bdot(mask_ref[at, :], table_ref[...]))
        spec += bdot(own_top[:, at], half_top)
        spec += bdot(own_top[:, at], half_low) + bdot(own_low[:, at], half_top)
    spec_out[...] = spec
    finish_low()
    rims[side] = pick(tile_count, held, pos_ref).astype(jnp.bfloat16)
    rim_copy = pltpu.make_async_remote_copy(
        src_ref=rims.at[side],
        dst_ref=rims.at[side],
        send_sem=send_r.at[0],
        recv_sem=recv_r.at[0],
        device_id={"src": src + 1 - 2 * side},
        device_id_type=MESH,
    )
    rim_copy.start()
    f_a = lax.broadcasted_iota(jnp.int32, (FREQ, FREQ), 0) - FREQ // 2
    f_b = lax.broadcasted_iota(jnp.int32, (FREQ, FREQ), 1) - FREQ // 2
    inside = f_a * f_a + f_b * f_b <= PUPIL_R * PUPIL_R
    pupil_out[0] = jnp.where(inside, jnp.cos(phase_ref[...]), 0.0)
    pupil_out[1] = jnp.where(inside, jnp.sin(phase_ref[...]), 0.0)
    for copy in meta_copies:
        copy.wait()
    meta_out[...] = meta_held[...]
    rim_copy.wait()
    rims_out[...] = rims[...]


def back_kernel(
    tile_count, pos_ref, grad_ref, row_table, out_ref,
    held, grads, total, send_a, recv_a, send_b, recv_b, send_s, recv_s, rim_table, own_table, load
):
    low, high = group_sizes(tile_count)
    tile = lax.axis_index("tile")
    src = lax.axis_index("src")
    src_count = lax.axis_size("src")
    rows = out_ref.shape[0]
    rim_at = pl.multiple_of((1 - src % 2) * (EXT_PX - HALO), HALO)
    own_at = pl.multiple_of(HALO + src * rows, HALO)
    rim_load = pltpu.make_async_copy(row_table.at[pl.ds(rim_at, HALO), :], rim_table, load.at[0])
    own_load = pltpu.make_async_copy(row_table.at[pl.ds(own_at, rows), :], own_table, load.at[1])
    rim_load.start()
    own_load.start()
    grads[src] = grad_ref[...]
    greet(tile_count)
    for copy in start_src(grads, send_s, recv_s):
        copy.wait()
    both = grads[0]
    for k in range(1, src_count):
        both = both + grads[k]
    total[:FREQ, :] = both
    total[FREQ:, :FREQ] = -both[:, FREQ:]
    total[FREQ:, FREQ:] = both[:, :FREQ]
    rim_load.wait()
    rim_back = fdot(rim_table[...], total[...], HIGHEST)
    held[tile % low, tile // low] = rim_back.astype(jnp.bfloat16)
    high_copies = start_high(tile_count, held, send_a, recv_a)
    own_load.wait()
    out_ref[...] = fdot(own_table[...], total[...], HIGHEST)
    for copy in high_copies:
        copy.wait()
    start_low(tile_count, held, send_b, recv_b)()
    block = pick(tile_count, held, pos_ref)
    first = jnp.where(src == 0, 1.0, 0.0)
    last = jnp.where(src == src_count - 1, 1.0, 0.0)
    out_ref[:HALO, :] += first * block
    out_ref[rows - HALO :, :] += last * block


def comm_scratch(tile_count):
    low, high = group_sizes(tile_count)
    dma = pltpu.SemaphoreType.DMA
    sems = [dma((max(high - 1, 1),))] * 2 + [dma((max(low - 1, 1),))] * 2 + [dma((max(lax.axis_size("src") - 1, 1),))] * 2
    held = pltpu.VMEM((low, high, HALO, 2 * FREQ), jnp.bfloat16)
    return held, sems


def exchange_rims(tile_count, slot_pos, src_shift, src_weight, mask_tiles, *tables):
    held, sems = comm_scratch(tile_count)
    block = (HALO, 2 * FREQ)
    metas = (lax.axis_size("src"), 8, 128)
    vmem = pl.BlockSpec(memory_space=pltpu.VMEM)
    smem = pl.BlockSpec(memory_space=pltpu.SMEM)
    hbm = pl.BlockSpec(memory_space=pl.ANY)
    return pl.pallas_call(
        functools.partial(rim_kernel, tile_count),
        out_shape=[
            jax.ShapeDtypeStruct((2, *block), jnp.bfloat16),
            jax.ShapeDtypeStruct(metas, jnp.int32),
            jax.ShapeDtypeStruct((2 * FREQ, 2 * FREQ), jnp.float32),
            jax.ShapeDtypeStruct((2, FREQ, FREQ), jnp.float32),
        ],
        in_specs=[smem, smem, smem, hbm, vmem, hbm, hbm, vmem],
        out_specs=[vmem] * 4,
        scratch_shapes=[
            held,
            pltpu.VMEM((2, *block), jnp.bfloat16),
            pltpu.VMEM(metas, jnp.int32),
            *sems,
            pltpu.SemaphoreType.DMA((1,)),
            pltpu.SemaphoreType.DMA((1,)),
            pltpu.VMEM((HALO, TILE_PX), jnp.bfloat16),
            pltpu.VMEM((TILE_PX, TILE_PX), jnp.bfloat16),
            pltpu.VMEM((2 * FREQ, TILE_PX), jnp.bfloat16),
            pltpu.VMEM((2 * FREQ, TILE_PX), jnp.bfloat16),
            pltpu.SemaphoreType.DMA((4,)),
        ],
        compiler_params=pltpu.CompilerParams(
            collective_id=0, has_side_effects=True, vmem_limit_bytes=56 * 2**20
        ),
        cost_estimate=pl.CostEstimate(flops=6 * 10**8, bytes_accessed=2**22, transcendentals=0),
    )(slot_pos, src_shift, src_weight, mask_tiles, *tables)


def split(value):
    top = value.astype(jnp.bfloat16)
    return top, (value - top.astype(jnp.float32)).astype(jnp.bfloat16)


def np_split(value):
    top = value.astype(jnp.bfloat16)
    return top, (value - top.astype(np.float32)).astype(jnp.bfloat16)


def bdot(left, right):
    return jnp.dot(left, right, preferred_element_type=jnp.float32)


def bdot_t(left, right):
    return lax.dot_general(
        left, right, (((1,), (1,)), ((), ())), preferred_element_type=jnp.float32
    )


def image_kernel(
    sources_total, scale_factor, place_ref, meta_ref,
    spec_ref, rims_ref, rim_top, rim_low, phase_ref, line_top, line_low,
    table_ref, table_t_ref, target_ref, resist_ref, grad_ref,
    pupil_re, pupil_im, amp_top, amp_low, fields, damps, dlines
):
    step = pl.program_id(0)
    width = target_ref.shape[2]

    @pl.when(step == 0)
    def _():
        rims = rims_ref[...].reshape(2 * HALO, 2 * FREQ)
        spec4 = spec_ref[...] + bdot(rim_top[...], rims) + bdot(rim_low[...], rims)
        spec_re = scale_factor * (spec4[:FREQ, :FREQ] - spec4[FREQ:, FREQ:])
        spec_im = -scale_factor * (spec4[:FREQ, FREQ:] + spec4[FREQ:, :FREQ])
        phase_re, phase_im = phase_ref[0], phase_ref[1]
        for s in range(sources_total):
            move_a = (FREQ - meta_ref[s // SRC_DEV, s % SRC_DEV, 0]) % FREQ
            move_b = (FREQ - meta_ref[s // SRC_DEV, s % SRC_DEV, 1]) % FREQ
            p_re = pltpu.roll(pltpu.roll(phase_re, move_a, 0), move_b, 1)
            p_im = pltpu.roll(pltpu.roll(phase_im, move_a, 0), move_b, 1)
            pupil_re[s] = p_re
            pupil_im[s] = p_im
            at = slice(s * FREQ, (s + 1) * FREQ)
            for part, value in (
                (slice(0, FREQ), p_re * spec_re - p_im * spec_im),
                (slice(FREQ, 2 * FREQ), p_re * spec_im + p_im * spec_re),
            ):
                top, low = split(value)
                amp_top[at, part] = top
                amp_low[at, part] = low
        damps[...] = jnp.zeros_like(damps)

    table = table_ref[...]
    intensity = jnp.zeros((table.shape[0], width), jnp.float32)
    weights = []
    for s in range(sources_total):
        weight = meta_ref[s // SRC_DEV, s % SRC_DEV, 2].astype(jnp.float32)
        weight = weight * (1.0 / (4.0 * sources_total))
        weights.append(weight)
        at = slice(s * FREQ, (s + 1) * FREQ)
        line = bdot(amp_top[at, :], line_top[...])
        line += bdot(amp_top[at, :], line_low[...]) + bdot(amp_low[at, :], line_top[...])
        re, im = line[:, :width].astype(jnp.bfloat16), line[:, width:].astype(jnp.bfloat16)
        field_re = bdot(table, jnp.concatenate([re, -im], axis=0))
        field_im = bdot(table, jnp.concatenate([im, re], axis=0))
        fields[s, :, :width] = field_re
        fields[s, :, width:] = field_im
        intensity += weight * (field_re * field_re + field_im * field_im)
    resist = 1.0 / (1.0 + jnp.exp(-steepness * (intensity - threshold)))
    resist_ref[0] = resist
    adjoint = 2.0 * (resist - target_ref[0].astype(jnp.float32)) * steepness
    adjoint = (adjoint * resist * (1.0 - resist)).astype(jnp.bfloat16).astype(jnp.float32)
    for s in range(sources_total):
        factor = 2.0 * weights[s] * adjoint
        d_re = (factor * fields[s, :, :width]).astype(jnp.bfloat16)
        d_im = (factor * fields[s, :, width:]).astype(jnp.bfloat16)
        b_re = bdot(table_t_ref[...], d_re)
        b_im = bdot(table_t_ref[...], d_im)
        at = slice(s * FREQ, (s + 1) * FREQ)
        dlines[at, :width] = (b_re[:FREQ] + b_im[FREQ:]).astype(jnp.bfloat16)
        dlines[at, width:] = (b_im[:FREQ] - b_re[FREQ:]).astype(jnp.bfloat16)
    damps[...] += bdot_t(dlines[...], line_top[...])

    @pl.when(step == pl.num_programs(0) - 1)
    def _():
        grad_re = jnp.zeros((FREQ, FREQ), jnp.float32)
        grad_im = jnp.zeros((FREQ, FREQ), jnp.float32)
        for s in range(sources_total):
            at = slice(s * FREQ, (s + 1) * FREQ)
            damp_re, damp_im = damps[at, :FREQ], damps[at, FREQ:]
            grad_re += pupil_re[s] * damp_re + pupil_im[s] * damp_im
            grad_im += pupil_re[s] * damp_im - pupil_im[s] * damp_re
        grad_ref[:, :FREQ] = scale_factor * grad_re
        grad_ref[:, FREQ:] = scale_factor * grad_im


def image_step(place, metas, spec, rims, row_tables, phase, lines, table, table_t, target, rows):
    sources_total = SRC_DEV * metas.shape[0]
    scale_factor = 1.0 / (FREQ / 2 * math.sqrt(EXT_PX * TILE_PX))
    width = 256
    wide = 2 * FREQ

    def whole(*shape):
        return pl.BlockSpec(shape, lambda j, place, meta: (0,) * len(shape))

    grid_spec = pltpu.PrefetchScalarGridSpec(
        num_scalar_prefetch=2,
        grid=(TILE_PX // width,),
        in_specs=[
            whole(wide, wide),
            whole(2, HALO, wide),
            whole(wide, 2 * HALO),
            whole(wide, 2 * HALO),
            whole(2, FREQ, FREQ),
            pl.BlockSpec((wide, 2 * width), lambda j, place, meta: (0, j)),
            pl.BlockSpec((wide, 2 * width), lambda j, place, meta: (0, j)),
            pl.BlockSpec((rows, wide), lambda j, place, meta: (place[0], 0)),
            pl.BlockSpec((wide, rows), lambda j, place, meta: (0, place[0])),
            pl.BlockSpec((1, rows, width), lambda j, place, meta: (0, place[0], j)),
        ],
        out_specs=[
            pl.BlockSpec((1, rows, width), lambda j, place, meta: (0, 0, j)),
            whole(FREQ, wide),
        ],
        scratch_shapes=[
            pltpu.VMEM((sources_total, FREQ, FREQ), jnp.float32),
            pltpu.VMEM((sources_total, FREQ, FREQ), jnp.float32),
            pltpu.VMEM((sources_total * FREQ, wide), jnp.bfloat16),
            pltpu.VMEM((sources_total * FREQ, wide), jnp.bfloat16),
            pltpu.VMEM((sources_total, rows, 2 * width), jnp.float32),
            pltpu.VMEM((sources_total * FREQ, wide), jnp.float32),
            pltpu.VMEM((sources_total * FREQ, 2 * width), jnp.bfloat16),
        ],
    )
    return pl.pallas_call(
        functools.partial(image_kernel, sources_total, scale_factor),
        grid_spec=grid_spec,
        out_shape=[
            jax.ShapeDtypeStruct((1, rows, TILE_PX), jnp.float32),
            jax.ShapeDtypeStruct((FREQ, wide), jnp.float32),
        ],
        compiler_params=pltpu.CompilerParams(vmem_limit_bytes=56 * 2**20),
        cost_estimate=pl.CostEstimate(flops=10**10, bytes_accessed=10**7, transcendentals=10**6),
    )(place, metas, spec, rims, *row_tables, phase, *lines, table, table_t, target)


def exchange_back(tile_count, slot_pos, grad, row_table, rows):
    held, sems = comm_scratch(tile_count)
    vmem = pl.BlockSpec(memory_space=pltpu.VMEM)
    return pl.pallas_call(
        functools.partial(back_kernel, tile_count),
        out_shape=jax.ShapeDtypeStruct((rows, 2 * FREQ), jnp.float32),
        in_specs=[
            pl.BlockSpec(memory_space=pltpu.SMEM), vmem, pl.BlockSpec(memory_space=pl.ANY)
        ],
        out_specs=vmem,
        scratch_shapes=[
            held,
            pltpu.VMEM((lax.axis_size("src"), *grad.shape), jnp.float32),
            pltpu.VMEM((2 * FREQ, 2 * FREQ), jnp.float32),
            *sems,
            pltpu.VMEM((HALO, 2 * FREQ), jnp.float32),
            pltpu.VMEM((rows, 2 * FREQ), jnp.float32),
            pltpu.SemaphoreType.DMA((2,)),
        ],
        compiler_params=pltpu.CompilerParams(
            collective_id=1, has_side_effects=True, vmem_limit_bytes=56 * 2**20
        ),
        cost_estimate=pl.CostEstimate(flops=10**8, bytes_accessed=2**21, transcendentals=0),
    )(slot_pos, grad, row_table)


def per_device(mask_tiles, slot_pos, src_shift, src_weight, pupil_phase, target):
    tile_count = lax.axis_size("tile")
    my_src = lax.axis_index("src")
    rows = TILE_PX // lax.axis_size("src")
    col_cos, col_sin = np_tables(np.arange(TILE_PX), TILE_PX)
    row_cos, row_sin = np_tables(np.arange(EXT_PX), EXT_PX)
    col_both = np.concatenate([col_cos, col_sin], axis=1).astype(jnp.bfloat16)
    last_table = np.concatenate([col_cos.T, -col_sin.T], axis=0).astype(jnp.bfloat16)
    line_table = np.stack(
        [
            np.concatenate([col_cos.T, -col_sin.T], axis=0).reshape(2 * FREQ, -1, 256),
            np.concatenate([col_sin.T, col_cos.T], axis=0).reshape(2 * FREQ, -1, 256),
        ],
        axis=2,
    ).reshape(2 * FREQ, 2 * TILE_PX)
    row_both = np.concatenate([row_cos, row_sin], axis=1)
    row_own = np.ascontiguousarray(row_both[HALO : HALO + TILE_PX].T)
    row_rim = np.concatenate([row_both[:HALO], row_both[EXT_PX - HALO :]], axis=0).T
    rim_tables = np_split(np.ascontiguousarray(row_rim))
    out_table = row_both[HALO : HALO + TILE_PX].astype(jnp.bfloat16)

    rims, metas, spec_own, pupil = exchange_rims(
        tile_count, slot_pos, src_shift, src_weight, mask_tiles, col_both,
        *np_split(row_own), pupil_phase
    )
    place = jnp.full((1,), my_src, jnp.int32)
    resist, grad = image_step(
        place, metas, spec_own, rims, rim_tables, pupil, np_split(line_table),
        out_table, np.ascontiguousarray(out_table.T), target, rows
    )
    back_rows = exchange_back(tile_count, slot_pos, grad, row_both, rows)
    step_rows = jnp.dot(
        back_rows.astype(jnp.bfloat16), last_table, preferred_element_type=jnp.float32
    )
    return (resist, (-learn_rate * step_rows)[None])


def solution(mesh):
    return jax.shard_map(
        per_device,
        mesh=mesh,
        in_specs=(P("tile", None, None), P(), P("src", None), P("src"), P(), P("tile", None, None)),
        out_specs=(P("tile", "src", None), P("tile", "src", None)),
        check_vma=False,
    )
```
